32 devices in a mesh: groups: 2 (over x), lat: 4 (over y, core), lon: 4 (over z).
Axes of the slice: x: 2, y: 2, z: 4, core: 2. Of those that a mesh axis runs over, the one named last changes fastest.
Arguments:
- fields: bfloat16 [256, 160, 69], P(('groups', 'lat'), 'lon'), parts along dimension 0, may hold values from -6 to 6
- first_kernel: bfloat16 [3, 3, 69, 256], replicated, may hold values from -0.25 to 0.25
- second_kernel: bfloat16 [3, 3, 256, 256], replicated, may hold values from -0.125 to 0.125
- down_weight: bfloat16 [4096, 1024], P(('lat', 'lon')), may hold values from -0.09375 to 0.09375
- projections: bfloat16 [1024, 3, 1024], replicated, may hold values from -0.1875 to 0.1875
- output_weight: bfloat16 [1024, 1024], replicated, may hold values from -0.1875 to 0.1875
Outputs:
- latent: bfloat16 [64, 40, 1024], P(('groups', 'lat', 'lon')), parts along dimension 0
The draws below stay inside these ranges and needn't reach their ends.
There are 2 independent parts, one for each index of `groups`. The reference program is written for one: setup_inputs(seed, part) draws one part's arguments, and reference() takes and returns one part's arrays. A program takes and returns all parts, laid end to end along the dimension named above; an argument that names none is the same for every part. Nothing has to cross between parts.
All inputs are finite; a program needn't handle non-finite values.
Results may differ from the reference program's by a relative error of at most 0.013.
Values may be sent and summed in bfloat16 or wider, within the bound.
A program may use at most 64 MiB of HBM per device.

```python
import jax
import jax.numpy as jnp
from jax import lax

CIN = 69
C = 256
D = 1024
HD = 64
LATS = 128
LONS = 160
TROWS = 32
TCOLS = 40


def shard_levels(own_key, shape, shards, smallest, high):
    loudness = 1.0
    for axis_at, parts in shards:
        steps = jax.random.uniform(jax.random.fold_in(jax.random.fold_in(own_key, 6), axis_at), (parts,), jnp.float32, smallest / len(shards), high / len(shards))
        loudness = loudness * jnp.repeat(jnp.exp(steps), shape[axis_at] // parts).reshape((-1,) + (1,) * (len(shape) - 1 - axis_at))
    return loudness


def noise(stream_key, shape, scale, limit, split=(), kind=jnp.bfloat16):
    drawn = jax.random.normal(stream_key, shape, jnp.float32) * scale
    if len(split) > 0:
        drawn = shard_levels(stream_key, shape, split, -0.22, 0.18) * drawn
    return jnp.clip(drawn, min=-limit, max=limit).astype(kind)


def setup_inputs(seed: int = 0, part: int = 0) -> dict:
    arg_keys = jax.random.split(jax.random.key(seed), 7)
    part_splits = jax.random.split(jax.random.fold_in(arg_keys[6], part), 7)
    fields = noise(part_splits[0], (LATS, LONS, CIN), 1.0, 6.0, ((0, 4), (1, 4)))
    first_kernel = noise(arg_keys[1], (3, 3, CIN, C), (9 * CIN) ** -0.5, 0.25)
    second_kernel = noise(arg_keys[2], (3, 3, C, C), (9 * C) ** -0.5, 0.125)
    down_weight = noise(arg_keys[3], (16 * C, D), (16 * C) ** -0.5, 0.09375, ((0, 16),))
    projections = noise(arg_keys[4], (D, 3, D), D ** -0.5, 0.1875)
    output_weight = noise(arg_keys[5], (D, D), D ** -0.5, 0.1875)
    return {"fields": fields, "first_kernel": first_kernel, "second_kernel": second_kernel, "down_weight": down_weight, "projections": projections, "output_weight": output_weight}


epsilon = 1e-05

def convolve(field, kernel):
    padded = jnp.pad(field, ((0, 0), (1, 1), (0, 0)), mode='wrap')
    padded = jnp.pad(padded, ((1, 1), (0, 0), (0, 0)))
    height, breadth = (field.shape[0], field.shape[1])
    total = jnp.zeros((height * breadth, kernel.shape[3]), jnp.float32)
    for row_shift in range(3):
        for col_shift in range(3):
            window = padded[row_shift:row_shift + height, col_shift:col_shift + breadth].reshape(height * breadth, -1)
            total = total + jnp.dot(window, kernel[row_shift, col_shift], preferred_element_type=jnp.float32)
    return total.reshape(height, breadth, -1)

def attention(band, query_weight, key_weight, value_weight):
    row_count, token_count = (band.shape[0], band.shape[1])
    widened = band.astype(jnp.float32)
    average = lax.optimization_barrier(jnp.mean(widened, axis=-1, keepdims=True))
    centred = widened - average
    spread = lax.optimization_barrier(jnp.mean(centred * centred, axis=-1, keepdims=True))
    normed = (centred * lax.rsqrt(spread + epsilon)).astype(jnp.bfloat16).reshape(row_count * token_count, -1)
    head_count = query_weight.shape[1] // HD

    def project(weight):
        return jnp.dot(normed, weight, preferred_element_type=jnp.float32).astype(jnp.bfloat16).reshape(row_count, token_count, head_count, HD)
    query = project(query_weight)
    keys = project(key_weight)
    values = project(value_weight)
    scores = jnp.einsum('rqhd,rkhd->rhqk', query.astype(jnp.float32), keys.astype(jnp.float32)) * HD ** (-0.5)
    probs = jax.nn.softmax(scores, axis=-1).astype(jnp.bfloat16)
    mixed = jnp.einsum('rhqk,rkhd->rqhd', probs.astype(jnp.float32), values.astype(jnp.float32)).astype(jnp.bfloat16)
    return mixed.reshape(row_count * token_count, head_count * HD)

def reference(fields, first_kernel, second_kernel, down_weight, projections, output_weight):
    first = jax.nn.gelu(convolve(fields, first_kernel)).astype(jnp.bfloat16)
    second = (first.astype(jnp.float32) + jax.nn.gelu(convolve(first, second_kernel))).astype(jnp.bfloat16)
    patches = second.reshape(TROWS, 4, TCOLS, 4, C).transpose(0, 2, 1, 3, 4).reshape(TROWS * TCOLS, 16 * C)
    tokens = jnp.dot(patches, down_weight, preferred_element_type=jnp.float32).astype(jnp.bfloat16).reshape(TROWS, TCOLS, D)

    def one_row(single):
        band = single[None]
        mixed = attention(band, projections[:, 0], projections[:, 1], projections[:, 2])
        summed = band.astype(jnp.float32).reshape(-1, D) + jnp.dot(mixed, output_weight, preferred_element_type=jnp.float32)
        return summed.astype(jnp.bfloat16)
    return lax.map(one_row, tokens)
```

```python
import jax
import jax.numpy as jnp
from jax import lax
from jax.sharding import PartitionSpec as P

C = 256
D = 1024
HD = 64


epsilon = 1e-05


def extended(cells, sides, width, closed):
    for axis, dim in sides:
        count = lax.axis_size(axis)
        ends = count if closed else count - 1
        head = lax.slice_in_dim(cells, 0, width, axis=dim)
        tail = lax.slice_in_dim(cells, cells.shape[dim] - width, cells.shape[dim], axis=dim)
        cells = jnp.concatenate(
            [
                lax.ppermute(tail, axis, [(i, (i + 1) % count) for i in range(ends)]),
                cells,
                lax.ppermute(head, axis, [((i + 1) % count, i) for i in range(ends)]),
            ],
            axis=dim,
        )
    return cells


def extend(field, margin):
    wider = extended(field, (("lat", 0),), margin, False)
    return extended(wider, (("lon", 1),), margin, True)


def convolve_tile(padded, kernel, row_count, col_count):
    total = jnp.zeros((row_count * col_count, kernel.shape[3]), jnp.float32)
    for row_shift in range(3):
        for col_shift in range(3):
            window = padded[
                row_shift : row_shift + row_count, col_shift : col_shift + col_count
            ].reshape(row_count * col_count, -1)
            total = total + jnp.dot(
                window, kernel[row_shift, col_shift], preferred_element_type=jnp.float32
            )
    return total.reshape(row_count, col_count, -1)


def attention(band, query_weight, key_weight, value_weight):
    row_count, token_count = (band.shape[0], band.shape[1])
    widened = band.astype(jnp.float32)
    average = jnp.mean(widened, axis=-1, keepdims=True)
    centred = widened - average
    spread = jnp.mean(centred * centred, axis=-1, keepdims=True)
    normed = (
        (centred * lax.rsqrt(spread + epsilon))
        .astype(jnp.bfloat16)
        .reshape(row_count * token_count, -1)
    )
    head_count = query_weight.shape[1] // HD

    def project(weight):
        return (
            jnp.dot(normed, weight, preferred_element_type=jnp.float32)
            .astype(jnp.bfloat16)
            .reshape(row_count, token_count, head_count, HD)
        )

    query = project(query_weight)
    keys = project(key_weight)
    values = project(value_weight)
    scores = jnp.einsum(
        "rqhd,rkhd->rhqk", query, keys, preferred_element_type=jnp.float32
    ) * HD ** (-0.5)
    probs = jax.nn.softmax(scores, axis=-1).astype(jnp.bfloat16)
    mixed = jnp.einsum("rhqk,rkhd->rqhd", probs, values, preferred_element_type=jnp.float32).astype(
        jnp.bfloat16
    )
    return mixed.reshape(row_count * token_count, head_count * HD)


def on_device(fields, first_kernel, second_kernel, down_weight, projections, output_weight):
    groups, lats = lax.axis_size("groups"), lax.axis_size("lat")
    part = D // groups
    half = lax.dynamic_slice_in_dim(down_weight, lax.axis_index("groups") * part, part, axis=1)
    weights = lax.all_gather(half, ("groups", "lon"), axis=0, tiled=True)
    row_count, col_count = (fields.shape[0], fields.shape[1])
    first = jax.nn.gelu(
        convolve_tile(extend(fields, 2), first_kernel, row_count + 2, col_count + 2)
    ).astype(jnp.bfloat16)
    lat = lax.axis_index("lat")
    row = lax.broadcasted_iota(jnp.int32, first.shape, 0)
    outside = ((row == 0) & (lat == 0)) | ((row == row_count + 1) & (lat == lats - 1))
    first = jnp.where(outside, jnp.zeros_like(first), first)
    middle = convolve_tile(first, second_kernel, row_count, col_count)
    own = first[1:-1, 1:-1]
    second = (own.astype(jnp.float32) + jax.nn.gelu(middle)).astype(jnp.bfloat16)
    token_rows, token_cols = (row_count // 4, col_count // 4)
    count = token_rows * token_cols
    depth = 16 * C // lats
    patches = (
        second.reshape(token_rows, 4, token_cols, 4, C)
        .transpose(1, 3, 0, 2, 4)
        .reshape(lats, 16 // lats, count, C)
    )
    patches = lax.all_to_all(patches, "lat", split_axis=0, concat_axis=0, tiled=True)
    patches = patches.transpose(0, 2, 1, 3).reshape(lats * count, depth)
    sums = jnp.concatenate(
        [
            jnp.dot(
                patches,
                weights[g * depth : (g + 1) * depth],
                preferred_element_type=jnp.float32,
            )
            for g in range(groups)
        ],
        axis=1,
    )
    sums = sums.astype(jnp.bfloat16).reshape(lats, count, D)
    sums = lax.all_to_all(sums, "lat", split_axis=0, concat_axis=0, tiled=True)
    tokens = jnp.sum(sums.astype(jnp.float32), axis=0)
    tokens = tokens.astype(jnp.bfloat16).reshape(token_rows, token_cols, D)
    band = lax.all_to_all(tokens, "lon", split_axis=0, concat_axis=1, tiled=True)
    mixed = attention(band, projections[:, 0], projections[:, 1], projections[:, 2])
    summed = band.astype(jnp.float32).reshape(-1, D) + jnp.dot(
        mixed, output_weight, preferred_element_type=jnp.float32
    )
    return summed.astype(jnp.bfloat16).reshape(band.shape)


def solution(mesh):
    placed = (P(("groups", "lat"), "lon", None), P(), P(), P(("lat", "lon"), None), P(), P())
    return jax.shard_map(
        on_device,
        mesh=mesh,
        in_specs=placed,
        out_specs=P(("groups", "lat", "lon"), None, None),
        check_vma=False,
    )
```

```python
import functools

import jax
import jax.numpy as jnp
from jax import lax
from jax.experimental import pallas as pl
from jax.experimental.pallas import tpu as pltpu
from jax.sharding import PartitionSpec as P

C = 256
D = 1024
HD = 64
WIDE = 48
LANES = 128
MESH = pl.DeviceIdType.MESH


epsilon = 1e-05

SIDES = [(da, db) for da in (-1, 0, 1) for db in (-1, 0, 1) if (da, db) != (0, 0)]


def side_rows(da, db, rows, cols):
    return (2 if da else rows) * (8 if db else cols)


def encode_kernel(
    sizes,
    fields,
    k1_ref,
    k2_hbm,
    down,
    band,
    x3,
    xb,
    f_ref,
    s_ref,
    t_ref,
    pb,
    pr,
    qb,
    qr,
    tok,
    tokpad,
    tb,
    wbuf,
    k2,
    *rest,
):
    groups, lats, lons, rows, cols = sizes
    out_halo, in_halo = rest[:8], rest[8:16]
    (
        local_sem,
        halo_send,
        halo_recv,
        z_send,
        z_recv,
        x_send,
        x_recv,
        p_send,
        p_recv,
        q_send,
        q_recv,
        t_send,
        t_recv,
    ) = rest[16:]
    g, a, b = lax.axis_index("groups"), lax.axis_index("lat"), lax.axis_index("lon")
    part = D // groups
    count = (rows // 4) * (cols // 4)
    depth = 16 * C // lats
    shard = depth // lons
    cnt = count // lons
    cp = -(-cnt // 16) * 16

    k2_copy = pltpu.make_async_copy(k2_hbm, k2, local_sem.at[0])
    k2_copy.start()
    own_copies = [
        pltpu.make_async_copy(
            down.at[:, pl.ds(h * part, part)], wbuf.at[h, b], local_sem.at[1 + h]
        )
        for h in range(groups)
    ]
    for copy in own_copies:
        copy.start()

    barrier = pltpu.get_barrier_semaphore()

    def greet(i, _):
        gg = i // (lats * lons)
        aa = (i // lons) % lats
        bb = i % lons
        pl.semaphore_signal(barrier, inc=1, device_id=(gg, aa, bb), device_id_type=MESH)
        return 0

    lax.fori_loop(0, groups * lats * lons, greet, 0)

    x3[...] = jnp.zeros(x3.shape, jnp.float32)
    x3[4 : 4 + rows, 0:cols, 0 : fields.shape[2]] = fields[...].astype(jnp.float32)
    for n, (da, db) in enumerate(SIDES):
        r0, r1 = {-1: (4, 6), 0: (4, 4 + rows), 1: (2 + rows, 4 + rows)}[da]
        c0, c1 = {-1: (0, 8), 0: (0, cols), 1: (cols - 8, cols)}[db]
        out_halo[n][...] = x3[r0:r1, c0:c1, :].reshape(-1, LANES).astype(jnp.bfloat16)

    pl.semaphore_wait(barrier, groups * lats * lons)

    def halo(n):
        da, db = SIDES[n]
        return pltpu.make_async_remote_copy(
            src_ref=out_halo[n],
            dst_ref=in_halo[n],
            send_sem=halo_send.at[n],
            recv_sem=halo_recv.at[n],
            device_id=(g, jnp.clip(a + da, 0, lats - 1), lax.rem(b + db + lons, lons)),
            device_id_type=MESH,
        )

    def inside(index):
        return jnp.logical_and(index >= 0, index < lats)

    for n, (da, db) in enumerate(SIDES):
        if da == 0:
            halo(n).start()
        else:

            @pl.when(inside(a + da))
            def _():
                halo(n).start()

    def along(c, step):
        return pltpu.make_async_remote_copy(
            src_ref=wbuf.at[g, c],
            dst_ref=wbuf.at[g, c],
            send_sem=z_send.at[c, (step + 1) // 2],
            recv_sem=z_recv.at[c],
            device_id=(g, a, jnp.clip(b + step, 0, lons - 1)),
            device_id_type=MESH,
        )

    def across(c, j):
        gg = lax.rem(g + j, groups)
        return pltpu.make_async_remote_copy(
            src_ref=wbuf.at[g, c],
            dst_ref=wbuf.at[g, c],
            send_sem=x_send.at[c, j],
            recv_sem=x_recv.at[g, c],
            device_id=(gg, a, b),
            device_id_type=MESH,
        )

    def relay(s):
        for way in (1, -1):
            c = b - way * s

            @pl.when(jnp.logical_and(c >= 0, c < lons))
            def _():
                if s > 0:
                    along(c, way).wait_recv()

                @pl.when(jnp.logical_and(b + way >= 0, b + way < lons))
                def _():
                    along(c, way).start()

                if s > 0:
                    for j in range(1, groups):
                        across(c, j).start()

    for copy in own_copies:
        copy.wait()
    relay(0)

    lane = lax.broadcasted_iota(jnp.int32, (1, 8, LANES), 1)
    for n, (da, db) in enumerate(SIDES):

        def place(n=n, da=da, db=db):
            halo(n).wait_recv()
            r0, nr = {-1: (4 + rows, 2), 0: (4, rows), 1: (2, 2)}[da]
            value = in_halo[n][...].astype(jnp.float32)
            if db == 0:
                x3[r0 : r0 + nr, 0:cols, :] = value.reshape(nr, cols, LANES)
            else:
                value = value.reshape(nr, 8, LANES)
                if db < 0:
                    value = jnp.where(lane < 2, value, 0.0)
                else:
                    value = jnp.where(lane >= 6, value, 0.0)
                    r0 = r0 - 1
                x3[r0 : r0 + nr, cols : cols + 8, :] = x3[r0 : r0 + nr, cols : cols + 8, :] + value

        if da == 0:
            place()
        else:
            pl.when(inside(a - da))(place)
    xb[...] = x3[...].reshape(-1, LANES).astype(jnp.bfloat16)

    def conv(source, start, size, weights):
        total = [None] * 3
        for dr in range(3):
            window = source[pl.ds(pl.multiple_of(start + dr * WIDE, 16), size), :]
            for dc in range(3):
                term = jnp.dot(window, weights(dr, dc), preferred_element_type=jnp.float32)
                total[dc] = term if total[dc] is None else total[dc] + term
        whole = pltpu.roll(total[0], 1, 0) + total[1] + pltpu.roll(total[2], size - 1, 0)
        return whole[16 : size - 16]

    f_ref[0:16, :] = jnp.zeros((16, C), jnp.bfloat16)
    tail = (rows + 3) * WIDE
    f_ref[tail + 16 : tail + 32, :] = jnp.zeros((16, C), jnp.bfloat16)
    lo = jnp.where(a == 0, 2 * WIDE - 4, -1)
    hi = jnp.where(a == lats - 1, (rows + 2) * WIDE - 4, tail)

    def first_step(k, _):
        size = 5 * WIDE
        value = jax.nn.gelu(
            conv(xb, (5 * k + 1) * WIDE - 16, size + 32, lambda r, c: k1_ref[3 * r + c])
        )
        at = k * size + lax.broadcasted_iota(jnp.int32, (size, C), 0)
        value = jnp.where(jnp.logical_and(at >= lo, at < hi), value, 0.0)
        f_ref[pl.ds(pl.multiple_of(16 + k * size, 16), size), :] = value.astype(jnp.bfloat16)
        return 0

    lax.fori_loop(0, (rows + 3) // 5, first_step, 0)
    relay(1)
    k2_copy.wait()

    def second_step(k, _):
        size = 4 * WIDE
        value = jax.nn.gelu(
            conv(f_ref, (4 * k + 1) * WIDE, size + 32, lambda r, c: k2[r, c])
        )
        own = f_ref[pl.ds(pl.multiple_of(16 + (4 * k + 2) * WIDE, 16), size), :]
        value = own.astype(jnp.float32) + value
        for h in range(C // LANES):
            s_ref[h, pl.ds(pl.multiple_of(k * size, 16), size), :] = value[
                :, h * LANES : (h + 1) * LANES
            ]
        return 0

    halfway = rows // 8
    lax.fori_loop(0, halfway, second_step, 0)
    if lons > 2:
        relay(2)
    lax.fori_loop(halfway, rows // 4, second_step, 0)
    for s in range(3, lons):
        relay(s)

    wide = cols // 4
    for t in range(rows // 4):
        for p in range(4):
            for q in range(4):
                at = (4 * t + p) * WIDE + q
                for h in range(C // LANES):
                    to = (4 * p + q) * C + h * LANES
                    t_ref[t * wide : (t + 1) * wide, to : to + LANES] = s_ref[
                        h, pl.ds(at, wide, stride=4), :
                    ]
    for c in range(lats):
        pb[c * count : (c + 1) * count, :] = t_ref[:, c * depth : (c + 1) * depth].astype(
            jnp.bfloat16
        )

    def rows_of(ref, index, size):
        return ref.at[pl.ds(pl.multiple_of(index * size, 16), size)]

    def exchange(src, dst, size, send, recv, me, count_of, axis):
        def copy(j, incoming=False):
            other = lax.rem(me + j, count_of)
            target = (g, other, b) if axis == "lat" else (g, a, other)
            sender = lax.rem(me + count_of - j, count_of) if incoming else me
            return pltpu.make_async_remote_copy(
                src_ref=rows_of(src, other, size),
                dst_ref=rows_of(dst, sender, size),
                send_sem=send.at[j],
                recv_sem=recv.at[j],
                device_id=target,
                device_id_type=MESH,
            )

        for j in range(1, count_of):
            copy(j).start()
        mine = pl.ds(pl.multiple_of(me * size, 16), size)
        dst[mine, :] = src[mine, :]
        return copy

    to_k = exchange(pb, pr, count, p_send, p_recv, a, lats, "lat")

    def all_across(do):
        for s in range(1, lons):
            for way in (1, -1):
                c = b - way * s

                @pl.when(jnp.logical_and(c >= 0, c < lons))
                def _():
                    do(c)

    def take(c):
        for j in range(1, groups):
            gg = lax.rem(g + j, groups)
            pltpu.make_async_remote_copy(
                src_ref=wbuf.at[gg, c],
                dst_ref=wbuf.at[gg, c],
                send_sem=x_send.at[c, j],
                recv_sem=x_recv.at[gg, c],
                device_id=(gg, a, b),
                device_id_type=MESH,
            ).wait_recv()

    all_across(take)
    for j in range(1, lats):
        to_k(j, True).wait_recv()
    block = min(part, 256)
    for h in range(groups):
        for n in range(0, part, block):
            total = None
            for c in range(lons):
                term = jnp.dot(
                    pr[:, c * shard : (c + 1) * shard],
                    wbuf[h, c, :, n : n + block],
                    preferred_element_type=jnp.float32,
                )
                total = term if total is None else total + term
            qb[:, h * part + n : h * part + n + block] = total.astype(jnp.bfloat16)
    back = exchange(qb, qr, count, q_send, q_recv, a, lats, "lat")
    tokpad[...] = jnp.zeros(tokpad.shape, jnp.float32)
    for j in range(1, lats):
        back(j, True).wait_recv()
    total = qr[0:count, :].astype(jnp.float32)
    for c in range(1, lats):
        total = total + qr[c * count : (c + 1) * count, :].astype(jnp.float32)
    tok[...] = total
    for c in range(lons):
        tokpad[c * cp : c * cp + cnt, :] = tok[c * cnt : (c + 1) * cnt, :]
    tb[...] = tokpad[...].astype(jnp.bfloat16)
    to_rows = exchange(tb, band, cp, t_send, t_recv, b, lons, "lon")
    for j in range(1, lons):
        to_rows(j, True).wait_recv()

    for n, (da, db) in enumerate(SIDES):
        if da == 0:
            halo(n).wait_send()
        else:

            @pl.when(inside(a + da))
            def _():
                halo(n).wait_send()

    for s in range(lons):
        for way in (1, -1):
            c = b - way * s

            @pl.when(jnp.logical_and(c >= 0, c < lons))
            def _():
                @pl.when(jnp.logical_and(b + way >= 0, b + way < lons))
                def _():
                    along(c, way).wait_send()

                if s > 0:
                    for j in range(1, groups):
                        across(c, j).wait_send()

    for j in range(1, lats):
        to_k(j).wait_send()
        back(j).wait_send()
    for j in range(1, lons):
        to_rows(j).wait_send()


def encode(fields, first_kernel, second_kernel, down_weight):
    groups, lats, lons = (lax.axis_size(name) for name in ("groups", "lat", "lon"))
    rows, cols = fields.shape[0], fields.shape[1]
    count = (rows // 4) * (cols // 4)
    depth = 16 * C // lats
    cnt = count // lons
    cp = -(-cnt // 16) * 16
    padded = jnp.pad(
        first_kernel.reshape(9, -1, C), ((0, 0), (0, LANES - first_kernel.shape[2]), (0, 0))
    )
    halos = [
        pltpu.VMEM((side_rows(da, db, rows, cols), LANES), jnp.bfloat16) for da, db in SIDES
    ]
    dma = pltpu.SemaphoreType.DMA
    vmem = pl.BlockSpec(memory_space=pltpu.VMEM)
    anywhere = pl.BlockSpec(memory_space=pl.ANY)
    bf16, f32 = jnp.bfloat16, jnp.float32
    return pl.pallas_call(
        functools.partial(encode_kernel, (groups, lats, lons, rows, cols)),
        out_shape=jax.ShapeDtypeStruct((lons * cp, D), bf16),
        in_specs=[vmem, vmem, anywhere, anywhere],
        out_specs=vmem,
        scratch_shapes=[
            pltpu.VMEM((rows + 7, WIDE, LANES), f32),
            pltpu.VMEM(((rows + 7) * WIDE, LANES), bf16),
            pltpu.VMEM(((rows + 3) * WIDE + 32, C), bf16),
            pltpu.VMEM((C // LANES, rows * WIDE, LANES), f32),
            pltpu.VMEM((count, 16 * C), f32),
            pltpu.VMEM((lats * count, depth), bf16),
            pltpu.VMEM((lats * count, depth), bf16),
            pltpu.VMEM((lats * count, D), bf16),
            pltpu.VMEM((lats * count, D), bf16),
            pltpu.VMEM((count, D), f32),
            pltpu.VMEM((lons * cp, D), f32),
            pltpu.VMEM((lons * cp, D), bf16),
            pltpu.VMEM((groups, lons, depth // lons, D // groups), bf16),
            pltpu.VMEM(second_kernel.shape, bf16),
            *halos,
            *halos,
            dma((1 + groups,)),
            dma((8,)),
            dma((8,)),
            dma((lons, 2)),
            dma((lons,)),
            dma((lons, groups)),
            dma((groups, lons)),
            dma((lats,)),
            dma((lats,)),
            dma((lats,)),
            dma((lats,)),
            dma((lons,)),
            dma((lons,)),
        ],
        compiler_params=pltpu.CompilerParams(
            collective_id=0, has_side_effects=True, vmem_limit_bytes=44 * 1024 * 1024
        ),
    )(fields, padded, second_kernel, down_weight)


def attention(band, query_weight, key_weight, value_weight):
    row_count, token_count = (band.shape[0], band.shape[1])
    widened = band.astype(jnp.float32)
    average = jnp.mean(widened, axis=-1, keepdims=True)
    centred = widened - average
    spread = jnp.mean(centred * centred, axis=-1, keepdims=True)
    normed = (
        (centred * lax.rsqrt(spread + epsilon))
        .astype(jnp.bfloat16)
        .reshape(row_count * token_count, -1)
    )
    head_count = query_weight.shape[1] // HD

    def project(weight):
        return (
            jnp.dot(normed, weight, preferred_element_type=jnp.float32)
            .astype(jnp.bfloat16)
            .reshape(row_count, token_count, head_count, HD)
        )

    query = project(query_weight)
    keys = project(key_weight)
    values = project(value_weight)
    scores = jnp.einsum(
        "rqhd,rkhd->rhqk", query, keys, preferred_element_type=jnp.float32
    ) * HD ** (-0.5)
    probs = jax.nn.softmax(scores, axis=-1).astype(jnp.bfloat16)
    mixed = jnp.einsum("rhqk,rkhd->rqhd", probs, values, preferred_element_type=jnp.float32).astype(
        jnp.bfloat16
    )
    return mixed.reshape(row_count * token_count, head_count * HD)


def on_device(fields, first_kernel, second_kernel, down_weight, projections, output_weight):
    lons = lax.axis_size("lon")
    wide = fields.shape[1] // 4
    rows = fields.shape[0] // 4 // lons
    band = encode(fields, first_kernel, second_kernel, down_weight)
    band = band.reshape(lons, -1, D)[:, : rows * wide].reshape(lons, rows, wide, D)
    band = band.transpose(1, 0, 2, 3).reshape(rows, lons * wide, D)
    mixed = attention(band, projections[:, 0], projections[:, 1], projections[:, 2])
    summed = band.astype(jnp.float32).reshape(-1, D) + jnp.dot(
        mixed, output_weight, preferred_element_type=jnp.float32
    )
    return summed.astype(jnp.bfloat16).reshape(band.shape)


def solution(mesh):
    placed = (P(("groups", "lat"), "lon", None), P(), P(), P(("lat", "lon"), None), P(), P())
    return jax.shard_map(
        on_device,
        mesh=mesh,
        in_specs=placed,
        out_specs=P(("groups", "lat", "lon"), None, None),
        check_vma=False,
    )
```

```python
import functools

import jax
import jax.numpy as jnp
from jax import lax
from jax.experimental import pallas as pl
from jax.experimental.pallas import tpu as pltpu
from jax.sharding import PartitionSpec as P

C = 256
D = 1024
HD = 64
WIDE = 48
LANES = 128
SUBS = 2
MESH = pl.DeviceIdType.MESH


epsilon = 1e-05

SIDES = [(da, db) for da in (-1, 0, 1) for db in (-1, 0, 1) if (da, db) != (0, 0)]


def side_rows(da, db, rows, cols):
    return (2 if da else rows) * (8 if db else cols)


def encode_kernel(
    sizes,
    fields_hbm,
    k1_hbm,
    k2_hbm,
    down,
    band,
    fields,
    k1_ref,
    x3,
    xb,
    f_ref,
    s_ref,
    t_ref,
    pb,
    pr,
    qb,
    qr,
    tok,
    tokpad,
    tb,
    wbuf,
    k2,
    *rest,
):
    groups, lats, lons, rows, cols = sizes
    out_halo, in_halo = rest[:8], rest[8:16]
    (
        local_sem,
        halo_send,
        halo_recv,
        z_send,
        z_recv,
        x_send,
        x_recv,
        p_send,
        p_recv,
        q_send,
        q_recv,
        t_send,
        t_recv,
    ) = rest[16:]
    g, a, b = lax.axis_index("groups"), lax.axis_index("lat"), lax.axis_index("lon")
    part = D // groups
    count = (rows // 4) * (cols // 4)
    depth = 16 * C // lats
    shard = depth // lons
    cnt = count // lons
    cp = -(-cnt // 16) * 16

    fields_copy = pltpu.make_async_copy(fields_hbm, fields, local_sem.at[groups + 1])
    fields_copy.start()
    own_copies = [
        pltpu.make_async_copy(
            down.at[:, pl.ds(h * part, part)], wbuf.at[h, b], local_sem.at[1 + h]
        )
        for h in range(groups)
    ]
    for copy in own_copies:
        copy.start()
    k1_copy = pltpu.make_async_copy(k1_hbm, k1_ref, local_sem.at[groups + 2])
    k1_copy.start()
    k2_copy = pltpu.make_async_copy(k2_hbm, k2, local_sem.at[0])
    k2_copy.start()

    barrier = pltpu.get_barrier_semaphore()

    def greet(i, _):
        gg = i // (lats * lons)
        aa = (i // lons) % lats
        bb = i % lons
        pl.semaphore_signal(barrier, inc=1, device_id=(gg, aa, bb), device_id_type=MESH)
        return 0

    lax.fori_loop(0, groups * lats * lons, greet, 0)

    x3[...] = jnp.zeros(x3.shape, jnp.float32)
    fields_copy.wait()
    x3[4 : 4 + rows, 0:cols, 0 : fields.shape[2]] = fields[...].astype(jnp.float32)
    for n, (da, db) in enumerate(SIDES):
        r0, r1 = {-1: (4, 6), 0: (4, 4 + rows), 1: (2 + rows, 4 + rows)}[da]
        c0, c1 = {-1: (0, 8), 0: (0, cols), 1: (cols - 8, cols)}[db]
        out_halo[n][...] = x3[r0:r1, c0:c1, :].reshape(-1, LANES).astype(jnp.bfloat16)

    pl.semaphore_wait(barrier, groups * lats * lons)

    def halo(n):
        da, db = SIDES[n]
        return pltpu.make_async_remote_copy(
            src_ref=out_halo[n],
            dst_ref=in_halo[n],
            send_sem=halo_send.at[n],
            recv_sem=halo_recv.at[n],
            device_id=(g, jnp.clip(a + da, 0, lats - 1), lax.rem(b + db + lons, lons)),
            device_id_type=MESH,
        )

    def inside(index):
        return jnp.logical_and(index >= 0, index < lats)

    for n, (da, db) in enumerate(SIDES):
        if da == 0:
            halo(n).start()
        else:

            @pl.when(inside(a + da))
            def _():
                halo(n).start()

    piece = shard // SUBS

    def some(h, c, u):
        return wbuf.at[h, c, pl.ds(u * piece, piece)]

    def along(c, u, step):
        return pltpu.make_async_remote_copy(
            src_ref=some(g, c, u),
            dst_ref=some(g, c, u),
            send_sem=z_send.at[c, u, (step + 1) // 2],
            recv_sem=z_recv.at[c, u],
            device_id=(g, a, jnp.clip(b + step, 0, lons - 1)),
            device_id_type=MESH,
        )

    def across(c, u, j, incoming=False):
        gg = lax.rem(g + j, groups)
        h = gg if incoming else g
        return pltpu.make_async_remote_copy(
            src_ref=some(h, c, u),
            dst_ref=some(h, c, u),
            send_sem=x_send.at[c, u, j],
            recv_sem=x_recv.at[h, c, u],
            device_id=(gg, a, b),
            device_id_type=MESH,
        )

    def relay(s):
        for u in range(SUBS):
            for way in (1, -1):
                c = b - way * s

                @pl.when(jnp.logical_and(c >= 0, c < lons))
                def _():
                    if s > 0:
                        along(c, u, way).wait_recv()

                    @pl.when(jnp.logical_and(b + way >= 0, b + way < lons))
                    def _():
                        along(c, u, way).start()

                    if s > 0:
                        for j in range(1, groups):
                            across(c, u, j).start()

    for copy in own_copies:
        copy.wait()
    relay(0)

    lane = lax.broadcasted_iota(jnp.int32, (1, 8, LANES), 1)
    for n, (da, db) in enumerate(SIDES):

        def place(n=n, da=da, db=db):
            halo(n).wait_recv()
            r0, nr = {-1: (4 + rows, 2), 0: (4, rows), 1: (2, 2)}[da]
            value = in_halo[n][...].astype(jnp.float32)
            if db == 0:
                x3[r0 : r0 + nr, 0:cols, :] = value.reshape(nr, cols, LANES)
            else:
                value = value.reshape(nr, 8, LANES)
                if db < 0:
                    value = jnp.where(lane < 2, value, 0.0)
                else:
                    value = jnp.where(lane >= 6, value, 0.0)
                    r0 = r0 - 1
                x3[r0 : r0 + nr, cols : cols + 8, :] = x3[r0 : r0 + nr, cols : cols + 8, :] + value

        if da == 0:
            place()
        else:
            pl.when(inside(a - da))(place)
    xb[...] = x3[...].reshape(-1, LANES).astype(jnp.bfloat16)

    def conv(source, start, size, weights, channels):
        total = [None] * 3
        for dr in range(3):
            window = source[pl.ds(pl.multiple_of(start + dr * WIDE, 16), size), 0:channels]
            for dc in range(3):
                term = jnp.dot(window, weights(dr, dc), preferred_element_type=jnp.float32)
                total[dc] = term if total[dc] is None else total[dc] + term
        whole = pltpu.roll(total[0], 1, 0) + total[1] + pltpu.roll(total[2], size - 1, 0)
        return whole[16 : size - 16]

    f_ref[0:16, :] = jnp.zeros((16, C), jnp.bfloat16)
    tail = (rows + 3) * WIDE
    f_ref[tail + 16 : tail + 32, :] = jnp.zeros((16, C), jnp.bfloat16)
    lo = jnp.where(a == 0, 2 * WIDE - 4, -1)
    hi = jnp.where(a == lats - 1, (rows + 2) * WIDE - 4, tail)

    def first_step(k, _):
        size = 5 * WIDE
        value = jax.nn.gelu(
            conv(xb, (5 * k + 1) * WIDE - 16, size + 32, lambda r, c: k1_ref[r, c], k1_ref.shape[2])
        )
        at = k * size + lax.broadcasted_iota(jnp.int32, (size, C), 0)
        value = jnp.where(jnp.logical_and(at >= lo, at < hi), value, 0.0)
        f_ref[pl.ds(pl.multiple_of(16 + k * size, 16), size), :] = value.astype(jnp.bfloat16)
        return 0

    k1_copy.wait()
    lax.fori_loop(0, (rows + 3) // 5, first_step, 0)
    relay(1)
    k2_copy.wait()

    def second_step(k, _):
        size = 4 * WIDE
        value = jax.nn.gelu(
            conv(f_ref, (4 * k + 1) * WIDE, size + 32, lambda r, c: k2[r, c], C)
        )
        own = f_ref[pl.ds(pl.multiple_of(16 + (4 * k + 2) * WIDE, 16), size), :]
        value = own.astype(jnp.float32) + value
        for h in range(C // LANES):
            s_ref[h, pl.ds(pl.multiple_of(k * size, 16), size), :] = value[
                :, h * LANES : (h + 1) * LANES
            ]
        return 0

    def rows_of(ref, start, size):
        return ref.at[pl.ds(pl.multiple_of(start, 16), size)]

    wide = cols // 4

    def to_k(i, j, incoming=False):
        other = lax.rem(a + j, lats)
        sender = lax.rem(a + lats - j, lats) if incoming else a
        return pltpu.make_async_remote_copy(
            src_ref=rows_of(pb, other * count + 16 * i, 16),
            dst_ref=rows_of(pr, sender * count + 16 * i, 16),
            send_sem=p_send.at[i, j],
            recv_sem=p_recv.at[i, j],
            device_id=(g, other, b),
            device_id_type=MESH,
        )

    chunks = count // 16
    done = 0
    for i in range(chunks):
        until = min(-(-16 * (i + 1) // wide), rows // 4)
        lax.fori_loop(done, until, second_step, 0)
        for t in range(done, until):
            for p in range(4):
                for q in range(4):
                    at = (4 * t + p) * WIDE + q
                    for h in range(C // LANES):
                        to = (4 * p + q) * C + h * LANES
                        t_ref[t * wide : (t + 1) * wide, to : to + LANES] = s_ref[
                            h, pl.ds(at, wide, stride=4), :
                        ]
        done = until
        for c in range(lats):
            pb[c * count + 16 * i : c * count + 16 * (i + 1), :] = t_ref[
                16 * i : 16 * (i + 1), c * depth : (c + 1) * depth
            ].astype(jnp.bfloat16)
        for j in range(1, lats):
            to_k(i, j).start()
    mine = pl.ds(pl.multiple_of(a * count, 16), count)
    pr[mine, :] = pb[mine, :]
    tokpad[...] = jnp.zeros(tokpad.shape, jnp.float32)
    for s in range(2, lons):
        relay(s)
    for i in range(chunks):
        for j in range(1, lats):
            to_k(i, j, True).wait_recv()

    def back(i, j, incoming=False):
        h = lax.rem(g + i, groups)
        other = lax.rem(a + j, lats)
        sender = lax.rem(a + lats - j, lats) if incoming else a
        return pltpu.make_async_remote_copy(
            src_ref=rows_of(qb.at[h], other * count, count),
            dst_ref=rows_of(qr.at[h], sender * count, count),
            send_sem=q_send.at[i, j],
            recv_sem=q_recv.at[h, j],
            device_id=(g, other, b),
            device_id_type=MESH,
        )

    block = min(part, 256)
    for i in range(groups):
        h = lax.rem(g + i, groups)
        if i > 0:
            for s in range(1, lons):
                for way in (1, -1):
                    c = b - way * s

                    @pl.when(jnp.logical_and(c >= 0, c < lons))
                    def _():
                        for u in range(SUBS):
                            across(c, u, i, True).wait_recv()

        for n in range(0, part, block):
            total = None
            for c in range(lons):
                term = jnp.dot(
                    pr[:, c * shard : (c + 1) * shard],
                    wbuf[h, c, :, n : n + block],
                    preferred_element_type=jnp.float32,
                )
                total = term if total is None else total + term
            qb[h, :, n : n + block] = total.astype(jnp.bfloat16)
        for j in range(1, lats):
            back(i, j).start()
        qr[h, mine, :] = qb[h, mine, :]

    def to_rows(i, j, incoming=False):
        h = lax.rem(g + i, groups)
        other = lax.rem(b + j, lons)
        sender = lax.rem(b + lons - j, lons) if incoming else b
        return pltpu.make_async_remote_copy(
            src_ref=rows_of(tb.at[h], other * cp, cp),
            dst_ref=rows_of(band.at[h], sender * cp, cp),
            send_sem=t_send.at[i, j],
            recv_sem=t_recv.at[h, j],
            device_id=(g, a, other),
            device_id_type=MESH,
        )

    own = pl.ds(pl.multiple_of(b * cp, 16), cp)
    for i in range(groups):
        h = lax.rem(g + i, groups)
        for j in range(1, lats):
            back(i, j, True).wait_recv()
        total = qr[h, 0:count, :].astype(jnp.float32)
        for c in range(1, lats):
            total = total + qr[h, c * count : (c + 1) * count, :].astype(jnp.float32)
        tok[...] = total
        for c in range(lons):
            tokpad[c * cp : c * cp + cnt, :] = tok[c * cnt : (c + 1) * cnt, :]
        tb[h, :, :] = tokpad[...].astype(jnp.bfloat16)
        for j in range(1, lons):
            to_rows(i, j).start()
        band[h, own, :] = tb[h, own, :]
    for i in range(groups):
        for j in range(1, lons):
            to_rows(i, j, True).wait_recv()

    for n, (da, db) in enumerate(SIDES):
        if da == 0:
            halo(n).wait_send()
        else:

            @pl.when(inside(a + da))
            def _():
                halo(n).wait_send()

    for s in range(lons):
        for way in (1, -1):
            c = b - way * s

            @pl.when(jnp.logical_and(c >= 0, c < lons))
            def _():
                for u in range(SUBS):

                    @pl.when(jnp.logical_and(b + way >= 0, b + way < lons))
                    def _():
                        along(c, u, way).wait_send()

                    if s > 0:
                        for j in range(1, groups):
                            across(c, u, j).wait_send()

    for j in range(1, lats):
        for i in range(chunks):
            to_k(i, j).wait_send()
        for i in range(groups):
            back(i, j).wait_send()
    for j in range(1, lons):
        for i in range(groups):
            to_rows(i, j).wait_send()


def encode(fields, first_kernel, second_kernel, down_weight):
    groups, lats, lons = (lax.axis_size(name) for name in ("groups", "lat", "lon"))
    rows, cols = fields.shape[0], fields.shape[1]
    count = (rows // 4) * (cols // 4)
    depth = 16 * C // lats
    cnt = count // lons
    cp = -(-cnt // 16) * 16
    halos = [
        pltpu.VMEM((side_rows(da, db, rows, cols), LANES), jnp.bfloat16) for da, db in SIDES
    ]
    dma = pltpu.SemaphoreType.DMA
    vmem = pl.BlockSpec(memory_space=pltpu.VMEM)
    hbm = pl.BlockSpec(memory_space=pltpu.HBM)
    bf16, f32 = jnp.bfloat16, jnp.float32
    return pl.pallas_call(
        functools.partial(encode_kernel, (groups, lats, lons, rows, cols)),
        out_shape=jax.ShapeDtypeStruct((groups, lons * cp, D // groups), bf16),
        in_specs=[hbm] * 4,
        out_specs=vmem,
        scratch_shapes=[
            pltpu.VMEM(fields.shape, bf16),
            pltpu.VMEM(first_kernel.shape, bf16),
            pltpu.VMEM((rows + 7, WIDE, LANES), f32),
            pltpu.VMEM(((rows + 7) * WIDE, LANES), bf16),
            pltpu.VMEM(((rows + 3) * WIDE + 32, C), bf16),
            pltpu.VMEM((C // LANES, rows * WIDE, LANES), f32),
            pltpu.VMEM((count, 16 * C), f32),
            pltpu.VMEM((lats * count, depth), bf16),
            pltpu.VMEM((lats * count, depth), bf16),
            pltpu.VMEM((groups, lats * count, D // groups), bf16),
            pltpu.VMEM((groups, lats * count, D // groups), bf16),
            pltpu.VMEM((count, D // groups), f32),
            pltpu.VMEM((lons * cp, D // groups), f32),
            pltpu.VMEM((groups, lons * cp, D // groups), bf16),
            pltpu.VMEM((groups, lons, depth // lons, D // groups), bf16),
            pltpu.VMEM(second_kernel.shape, bf16),
            *halos,
            *halos,
            dma((3 + groups,)),
            dma((8,)),
            dma((8,)),
            dma((lons, SUBS, 2)),
            dma((lons, SUBS)),
            dma((lons, SUBS, groups)),
            dma((groups, lons, SUBS)),
            dma((count // 16, lats)),
            dma((count // 16, lats)),
            dma((groups, lats)),
            dma((groups, lats)),
            dma((groups, lons)),
            dma((groups, lons)),
        ],
        compiler_params=pltpu.CompilerParams(
            collective_id=0, has_side_effects=True, vmem_limit_bytes=44 * 1024 * 1024
        ),
    )(fields, first_kernel, second_kernel, down_weight)


def attention(band, query_weight, key_weight, value_weight):
    row_count, token_count = (band.shape[0], band.shape[1])
    widened = band.astype(jnp.float32)
    average = jnp.mean(widened, axis=-1, keepdims=True)
    centred = widened - average
    spread = jnp.mean(centred * centred, axis=-1, keepdims=True)
    normed = (
        (centred * lax.rsqrt(spread + epsilon))
        .astype(jnp.bfloat16)
        .reshape(row_count * token_count, -1)
    )
    head_count = query_weight.shape[1] // HD

    def project(weight):
        return (
            jnp.dot(normed, weight, preferred_element_type=jnp.float32)
            .astype(jnp.bfloat16)
            .reshape(row_count, token_count, head_count, HD)
        )

    query = project(query_weight)
    keys = project(key_weight)
    values = project(value_weight)
    scores = jnp.einsum(
        "rqhd,rkhd->rhqk", query, keys, preferred_element_type=jnp.float32
    ) * HD ** (-0.5)
    probs = jax.nn.softmax(scores, axis=-1).astype(jnp.bfloat16)
    mixed = jnp.einsum("rhqk,rkhd->rqhd", probs, values, preferred_element_type=jnp.float32).astype(
        jnp.bfloat16
    )
    return mixed.reshape(row_count * token_count, head_count * HD)


def on_device(fields, first_kernel, second_kernel, down_weight, projections, output_weight):
    lons = lax.axis_size("lon")
    wide = fields.shape[1] // 4
    rows = fields.shape[0] // 4 // lons
    band = encode(fields, first_kernel, second_kernel, down_weight)
    band = jnp.concatenate([band[h] for h in range(band.shape[0])], axis=1)
    band = band.reshape(lons, -1, D)[:, : rows * wide].reshape(lons, rows, wide, D)
    band = band.transpose(1, 0, 2, 3).reshape(rows, lons * wide, D)
    mixed = attention(band, projections[:, 0], projections[:, 1], projections[:, 2])
    summed = band.astype(jnp.float32).reshape(-1, D) + jnp.dot(
        mixed, output_weight, preferred_element_type=jnp.float32
    )
    return summed.astype(jnp.bfloat16).reshape(band.shape)


def solution(mesh):
    placed = (P(("groups", "lat"), "lon", None), P(), P(), P(("lat", "lon"), None), P(), P())
    return jax.shard_map(
        on_device,
        mesh=mesh,
        in_specs=placed,
        out_specs=P(("groups", "lat", "lon"), None, None),
        check_vma=False,
    )
```

```python
import functools

import jax
import jax.numpy as jnp
from jax import lax
from jax.experimental import pallas as pl
from jax.experimental.pallas import tpu as pltpu
from jax.sharding import PartitionSpec as P

C = 256
D = 1024
HD = 64
WIDE = 48
LANES = 128
SUBS = 2
VMEM_BYTES = 62 * 1024 * 1024
MESH = pl.DeviceIdType.MESH


epsilon = 1e-05

SIDES = [(da, db) for da in (-1, 0, 1) for db in (-1, 0, 1) if (da, db) != (0, 0)]


def side_rows(da, db, rows, cols):
    return (2 if da else rows) * (8 if db else cols)


def encode_kernel(
    sizes,
    fields_hbm,
    k1_hbm,
    k2_hbm,
    down,
    band,
    fields,
    k1_ref,
    x3,
    xb,
    f_ref,
    s_ref,
    t_ref,
    pb,
    pr,
    qb,
    qr,
    tok,
    tokpad,
    tb,
    wbuf,
    k2,
    *rest,
):
    groups, lats, lons, rows, cols = sizes
    out_halo, in_halo = rest[:8], rest[8:16]
    (
        local_sem,
        halo_send,
        halo_recv,
        z_send,
        z_recv,
        x_send,
        x_recv,
        p_send,
        p_recv,
        q_send,
        q_recv,
        t_send,
        t_recv,
    ) = rest[16:]
    g, a, b = lax.axis_index("groups"), lax.axis_index("lat"), lax.axis_index("lon")
    part = D // groups
    count = (rows // 4) * (cols // 4)
    depth = 16 * C // lats
    shard = depth // lons
    cnt = count // lons
    cp = -(-cnt // 16) * 16

    fields_copy = pltpu.make_async_copy(fields_hbm, fields, local_sem.at[groups + 1])
    fields_copy.start()
    own_copies = [
        pltpu.make_async_copy(
            down.at[:, pl.ds(h * part, part)], wbuf.at[h, b], local_sem.at[1 + h]
        )
        for h in range(groups)
    ]
    for copy in own_copies:
        copy.start()
    k1_copy = pltpu.make_async_copy(k1_hbm, k1_ref, local_sem.at[groups + 2])
    k1_copy.start()
    k2_copy = pltpu.make_async_copy(k2_hbm, k2, local_sem.at[0])
    k2_copy.start()

    barrier = pltpu.get_barrier_semaphore()

    def greet(device):
        pl.semaphore_signal(barrier, inc=1, device_id=device, device_id_type=MESH)

    for j in range(1, lats):
        greet((g, lax.rem(a + j, lats), b))
    for j in range(1, lons):
        greet((g, a, lax.rem(b + j, lons)))
    for j in range(1, groups):
        greet((lax.rem(g + j, groups), a, b))
    for da in (-1, 1):
        for db in (-1, 1):
            greet((g, lax.rem(a + da + lats, lats), lax.rem(b + db + lons, lons)))

    x3[...] = jnp.zeros(x3.shape, jnp.float32)
    fields_copy.wait()
    x3[4 : 4 + rows, 0:cols, 0 : fields.shape[2]] = fields[...].astype(jnp.float32)
    for n, (da, db) in enumerate(SIDES):
        r0, r1 = {-1: (4, 6), 0: (4, 4 + rows), 1: (2 + rows, 4 + rows)}[da]
        c0, c1 = {-1: (0, 8), 0: (0, cols), 1: (cols - 8, cols)}[db]
        out_halo[n][...] = x3[r0:r1, c0:c1, :].reshape(-1, LANES).astype(jnp.bfloat16)

    pl.semaphore_wait(barrier, lats + lons + groups + 1)

    def halo(n):
        da, db = SIDES[n]
        return pltpu.make_async_remote_copy(
            src_ref=out_halo[n],
            dst_ref=in_halo[n],
            send_sem=halo_send.at[n],
            recv_sem=halo_recv.at[n],
            device_id=(g, jnp.clip(a + da, 0, lats - 1), lax.rem(b + db + lons, lons)),
            device_id_type=MESH,
        )

    def inside(index):
        return jnp.logical_and(index >= 0, index < lats)

    for n, (da, db) in enumerate(SIDES):
        if da == 0:
            halo(n).start()
        else:

            @pl.when(inside(a + da))
            def _():
                halo(n).start()

    piece = shard // SUBS

    def some(h, c, u):
        return wbuf.at[h, c, pl.ds(u * piece, piece)]

    def along(c, u, step):
        return pltpu.make_async_remote_copy(
            src_ref=some(g, c, u),
            dst_ref=some(g, c, u),
            send_sem=z_send.at[c, u, (step + 1) // 2],
            recv_sem=z_recv.at[c, u],
            device_id=(g, a, jnp.clip(b + step, 0, lons - 1)),
            device_id_type=MESH,
        )

    def across(c, u, j, incoming=False):
        gg = lax.rem(g + j, groups)
        h = gg if incoming else g
        return pltpu.make_async_remote_copy(
            src_ref=some(h, c, u),
            dst_ref=some(h, c, u),
            send_sem=x_send.at[c, u, j],
            recv_sem=x_recv.at[h, c, u],
            device_id=(gg, a, b),
            device_id_type=MESH,
        )

    def relay(s):
        for u in range(SUBS):
            for way in (1, -1):
                c = b - way * s

                @pl.when(jnp.logical_and(c >= 0, c < lons))
                def _():
                    if s > 0:
                        along(c, u, way).wait_recv()

                    @pl.when(jnp.logical_and(b + way >= 0, b + way < lons))
                    def _():
                        along(c, u, way).start()

                    if s > 0:
                        for j in range(1, groups):
                            across(c, u, j).start()

    for copy in own_copies:
        copy.wait()
    relay(0)

    lane = lax.broadcasted_iota(jnp.int32, (1, 8, LANES), 1)
    for n, (da, db) in enumerate(SIDES):

        def place(n=n, da=da, db=db):
            halo(n).wait_recv()
            r0, nr = {-1: (4 + rows, 2), 0: (4, rows), 1: (2, 2)}[da]
            value = in_halo[n][...].astype(jnp.float32)
            if db == 0:
                x3[r0 : r0 + nr, 0:cols, :] = value.reshape(nr, cols, LANES)
            else:
                value = value.reshape(nr, 8, LANES)
                if db < 0:
                    value = jnp.where(lane < 2, value, 0.0)
                else:
                    value = jnp.where(lane >= 6, value, 0.0)
                    r0 = r0 - 1
                x3[r0 : r0 + nr, cols : cols + 8, :] = x3[r0 : r0 + nr, cols : cols + 8, :] + value

        if da == 0:
            place()
        else:
            pl.when(inside(a - da))(place)
    xb[...] = x3[...].reshape(-1, LANES).astype(jnp.bfloat16)

    def conv(source, start, size, weights, channels):
        total = [None] * 3
        for dr in range(3):
            window = source[pl.ds(pl.multiple_of(start + dr * WIDE, 16), size), 0:channels]
            for dc in range(3):
                term = jnp.dot(window, weights(dr, dc), preferred_element_type=jnp.float32)
                total[dc] = term if total[dc] is None else total[dc] + term
        whole = pltpu.roll(total[0], 1, 0) + total[1] + pltpu.roll(total[2], size - 1, 0)
        return whole[16 : size - 16]

    f_ref[0:16, :] = jnp.zeros((16, C), jnp.bfloat16)
    tail = (rows + 3) * WIDE
    f_ref[tail + 16 : tail + 32, :] = jnp.zeros((16, C), jnp.bfloat16)
    lo = jnp.where(a == 0, 2 * WIDE - 4, -1)
    hi = jnp.where(a == lats - 1, (rows + 2) * WIDE - 4, tail)

    def first_step(k, _):
        size = 5 * WIDE
        value = jax.nn.gelu(
            conv(xb, (5 * k + 1) * WIDE - 16, size + 32, lambda r, c: k1_ref[r, c], k1_ref.shape[2])
        )
        at = k * size + lax.broadcasted_iota(jnp.int32, (size, C), 0)
        value = jnp.where(jnp.logical_and(at >= lo, at < hi), value, 0.0)
        f_ref[pl.ds(pl.multiple_of(16 + k * size, 16), size), :] = value.astype(jnp.bfloat16)
        return 0

    k1_copy.wait()
    lax.fori_loop(0, (rows + 3) // 5, first_step, 0)
    relay(1)
    k2_copy.wait()

    def second_step(k, _):
        size = 4 * WIDE
        value = jax.nn.gelu(
            conv(f_ref, (4 * k + 1) * WIDE, size + 32, lambda r, c: k2[r, c], C)
        )
        own = f_ref[pl.ds(pl.multiple_of(16 + (4 * k + 2) * WIDE, 16), size), :]
        value = own.astype(jnp.float32) + value
        for h in range(C // LANES):
            s_ref[h, pl.ds(pl.multiple_of(k * size, 16), size), :] = value[
                :, h * LANES : (h + 1) * LANES
            ]
        return 0

    def rows_of(ref, start, size):
        return ref.at[pl.ds(pl.multiple_of(start, 16), size)]

    wide = cols // 4

    def to_k(i, j, incoming=False):
        other = lax.rem(a + j, lats)
        sender = lax.rem(a + lats - j, lats) if incoming else a
        return pltpu.make_async_remote_copy(
            src_ref=rows_of(pb, other * count + 16 * i, 16),
            dst_ref=rows_of(pr, sender * count + 16 * i, 16),
            send_sem=p_send.at[i, j],
            recv_sem=p_recv.at[i, j],
            device_id=(g, other, b),
            device_id_type=MESH,
        )

    chunks = count // 16
    done = 0
    for i in range(chunks):
        until = min(-(-16 * (i + 1) // wide), rows // 4)
        lax.fori_loop(done, until, second_step, 0)
        for t in range(done, until):
            for p in range(4):
                for q in range(4):
                    at = (4 * t + p) * WIDE + q
                    for h in range(C // LANES):
                        to = (4 * p + q) * C + h * LANES
                        t_ref[t * wide : (t + 1) * wide, to : to + LANES] = s_ref[
                            h, pl.ds(at, wide, stride=4), :
                        ]
        done = until
        for c in range(lats):
            pb[c * count + 16 * i : c * count + 16 * (i + 1), :] = t_ref[
                16 * i : 16 * (i + 1), c * depth : (c + 1) * depth
            ].astype(jnp.bfloat16)
        for j in range(1, lats):
            to_k(i, j).start()
    mine = pl.ds(pl.multiple_of(a * count, 16), count)
    pr[mine, :] = pb[mine, :]
    tokpad[...] = jnp.zeros(tokpad.shape, jnp.float32)
    for s in range(2, lons):
        relay(s)
    for i in range(chunks):
        for j in range(1, lats):
            to_k(i, j, True).wait_recv()

    def back(i, j, incoming=False):
        h = lax.rem(g + i, groups)
        other = lax.rem(a + j, lats)
        sender = lax.rem(a + lats - j, lats) if incoming else a
        return pltpu.make_async_remote_copy(
            src_ref=rows_of(qb.at[h], other * count, count),
            dst_ref=rows_of(qr.at[h], sender * count, count),
            send_sem=q_send.at[i, j],
            recv_sem=q_recv.at[h, j],
            device_id=(g, other, b),
            device_id_type=MESH,
        )

    block = min(part, 256)
    for i in range(groups):
        h = lax.rem(g + i, groups)
        if i > 0:
            for s in range(1, lons):
                for way in (1, -1):
                    c = b - way * s

                    @pl.when(jnp.logical_and(c >= 0, c < lons))
                    def _():
                        for u in range(SUBS):
                            across(c, u, i, True).wait_recv()

        for n in range(0, part, block):
            total = None
            for c in range(lons):
                term = jnp.dot(
                    pr[:, c * shard : (c + 1) * shard],
                    wbuf[h, c, :, n : n + block],
                    preferred_element_type=jnp.float32,
                )
                total = term if total is None else total + term
            qb[h, :, n : n + block] = total.astype(jnp.bfloat16)
        for j in range(1, lats):
            back(i, j).start()
        qr[h, mine, :] = qb[h, mine, :]

    def to_rows(i, j, incoming=False):
        h = lax.rem(g + i, groups)
        other = lax.rem(b + j, lons)
        sender = lax.rem(b + lons - j, lons) if incoming else b
        return pltpu.make_async_remote_copy(
            src_ref=rows_of(tb.at[h], other * cp, cp),
            dst_ref=rows_of(band.at[h], sender * cp, cp),
            send_sem=t_send.at[i, j],
            recv_sem=t_recv.at[h, j],
            device_id=(g, a, other),
            device_id_type=MESH,
        )

    own = pl.ds(pl.multiple_of(b * cp, 16), cp)
    for i in range(groups):
        h = lax.rem(g + i, groups)
        for j in range(1, lats):
            back(i, j, True).wait_recv()
        total = qr[h, 0:count, :].astype(jnp.float32)
        for c in range(1, lats):
            total = total + qr[h, c * count : (c + 1) * count, :].astype(jnp.float32)
        tok[...] = total
        for c in range(lons):
            tokpad[c * cp : c * cp + cnt, :] = tok[c * cnt : (c + 1) * cnt, :]
        tb[h, :, :] = tokpad[...].astype(jnp.bfloat16)
        for j in range(1, lons):
            to_rows(i, j).start()
        band[h, own, :] = tb[h, own, :]
    for i in range(groups):
        for j in range(1, lons):
            to_rows(i, j, True).wait_recv()

    for n, (da, db) in enumerate(SIDES):
        if da == 0:
            halo(n).wait_send()
        else:

            @pl.when(inside(a + da))
            def _():
                halo(n).wait_send()

    for s in range(lons):
        for way in (1, -1):
            c = b - way * s

            @pl.when(jnp.logical_and(c >= 0, c < lons))
            def _():
                for u in range(SUBS):

                    @pl.when(jnp.logical_and(b + way >= 0, b + way < lons))
                    def _():
                        along(c, u, way).wait_send()

                    if s > 0:
                        for j in range(1, groups):
                            across(c, u, j).wait_send()

    for j in range(1, lats):
        for i in range(chunks):
            to_k(i, j).wait_send()
        for i in range(groups):
            back(i, j).wait_send()
    for j in range(1, lons):
        for i in range(groups):
            to_rows(i, j).wait_send()


def encode(fields, first_kernel, second_kernel, down_weight):
    groups, lats, lons = (lax.axis_size(name) for name in ("groups", "lat", "lon"))
    rows, cols = fields.shape[0], fields.shape[1]
    count = (rows // 4) * (cols // 4)
    depth = 16 * C // lats
    cnt = count // lons
    cp = -(-cnt // 16) * 16
    halos = [
        pltpu.VMEM((side_rows(da, db, rows, cols), LANES), jnp.bfloat16) for da, db in SIDES
    ]
    dma = pltpu.SemaphoreType.DMA
    vmem = pl.BlockSpec(memory_space=pltpu.VMEM)
    hbm = pl.BlockSpec(memory_space=pltpu.HBM)
    bf16, f32 = jnp.bfloat16, jnp.float32
    return pl.pallas_call(
        functools.partial(encode_kernel, (groups, lats, lons, rows, cols)),
        out_shape=jax.ShapeDtypeStruct((groups, lons * cp, D // groups), bf16),
        in_specs=[hbm] * 4,
        out_specs=vmem,
        scratch_shapes=[
            pltpu.VMEM(fields.shape, bf16),
            pltpu.VMEM(first_kernel.shape, bf16),
            pltpu.VMEM((rows + 7, WIDE, LANES), f32),
            pltpu.VMEM(((rows + 7) * WIDE, LANES), bf16),
            pltpu.VMEM(((rows + 3) * WIDE + 32, C), bf16),
            pltpu.VMEM((C // LANES, rows * WIDE, LANES), f32),
            pltpu.VMEM((count, 16 * C), f32),
            pltpu.VMEM((lats * count, depth), bf16),
            pltpu.VMEM((lats * count, depth), bf16),
            pltpu.VMEM((groups, lats * count, D // groups), bf16),
            pltpu.VMEM((groups, lats * count, D // groups), bf16),
            pltpu.VMEM((count, D // groups), f32),
            pltpu.VMEM((lons * cp, D // groups), f32),
            pltpu.VMEM((groups, lons * cp, D // groups), bf16),
            pltpu.VMEM((groups, lons, depth // lons, D // groups), bf16),
            pltpu.VMEM(second_kernel.shape, bf16),
            *halos,
            *halos,
            dma((3 + groups,)),
            dma((8,)),
            dma((8,)),
            dma((lons, SUBS, 2)),
            dma((lons, SUBS)),
            dma((lons, SUBS, groups)),
            dma((groups, lons, SUBS)),
            dma((count // 16, lats)),
            dma((count // 16, lats)),
            dma((groups, lats)),
            dma((groups, lats)),
            dma((groups, lons)),
            dma((groups, lons)),
        ],
        compiler_params=pltpu.CompilerParams(
            collective_id=0, has_side_effects=True, vmem_limit_bytes=VMEM_BYTES
        ),
    )(fields, first_kernel, second_kernel, down_weight)


def project_all(band, query_weight, key_weight, value_weight):
    row_count, token_count = (band.shape[0], band.shape[1])
    widened = band.astype(jnp.float32)
    average = jnp.mean(widened, axis=-1, keepdims=True)
    centred = widened - average
    spread = jnp.mean(centred * centred, axis=-1, keepdims=True)
    normed = (
        (centred * lax.rsqrt(spread + epsilon))
        .astype(jnp.bfloat16)
        .reshape(row_count * token_count, -1)
    )
    def project(weight):
        return jnp.dot(normed, weight, preferred_element_type=jnp.float32).astype(jnp.bfloat16)

    return project(query_weight), project(key_weight), project(value_weight)


def mix_kernel(keys_in_row, query, keys, values, band, output_weight, out, mixed):
    count = query.shape[0]
    at = [lax.broadcasted_iota(jnp.int32, (count, count), dim) for dim in (0, 1)]
    same = None
    for r in range(count // keys_in_row):
        lo, hi = r * keys_in_row, (r + 1) * keys_in_row
        both = (at[0] >= lo) & (at[0] < hi) & (at[1] >= lo) & (at[1] < hi)
        same = both if same is None else same | both
    for n in range(query.shape[1] // HD):
        head = slice(n * HD, (n + 1) * HD)
        scores = lax.dot_general(
            query[:, head],
            keys[:, head],
            (((1,), (1,)), ((), ())),
            preferred_element_type=jnp.float32,
        ) * HD ** (-0.5)
        scores = jnp.where(same, scores, -jnp.inf)
        powers = jnp.exp(scores - jnp.max(scores, axis=-1, keepdims=True))
        probs = (powers / jnp.sum(powers, axis=-1, keepdims=True)).astype(jnp.bfloat16)
        mixed[:, head] = jnp.dot(
            probs, values[:, head], preferred_element_type=jnp.float32
        ).astype(jnp.bfloat16)
    for n in range(0, D, 256):
        out[:, n : n + 256] = (
            band[:, n : n + 256].astype(jnp.float32)
            + jnp.dot(
                mixed[...], output_weight[:, n : n + 256], preferred_element_type=jnp.float32
            )
        ).astype(jnp.bfloat16)


def on_device(fields, first_kernel, second_kernel, down_weight, projections, output_weight):
    lons = lax.axis_size("lon")
    wide = fields.shape[1] // 4
    rows = fields.shape[0] // 4 // lons
    band = encode(fields, first_kernel, second_kernel, down_weight)
    band = jnp.concatenate([band[h] for h in range(band.shape[0])], axis=1)
    band = band.reshape(lons, -1, D)[:, : rows * wide].reshape(lons, rows, wide, D)
    band = band.transpose(1, 0, 2, 3).reshape(rows, lons * wide, D)
    query, keys, values = project_all(
        band, projections[:, 0], projections[:, 1], projections[:, 2]
    )
    flat = band.reshape(-1, D)
    latent = pl.pallas_call(
        functools.partial(mix_kernel, lons * wide),
        out_shape=jax.ShapeDtypeStruct(flat.shape, jnp.bfloat16),
        in_specs=[pl.BlockSpec(memory_space=pltpu.VMEM)] * 5,
        out_specs=pl.BlockSpec(memory_space=pltpu.VMEM),
        scratch_shapes=[pltpu.VMEM(flat.shape, jnp.bfloat16)],
        compiler_params=pltpu.CompilerParams(vmem_limit_bytes=16 * 1024 * 1024),
    )(query, keys, values, flat, output_weight)
    return latent.reshape(band.shape)


def solution(mesh):
    placed = (P(("groups", "lat"), "lon", None), P(), P(), P(("lat", "lon"), None), P(), P())
    return jax.shard_map(
        on_device,
        mesh=mesh,
        in_specs=placed,
        out_specs=P(("groups", "lat", "lon"), None, None),
        check_vma=False,
    )
```
